32 devices in a mesh: groups: 2 (over y), rows: 4 (over z), angle: 4 (over x, core).
Axes of the slice: x: 2, y: 2, z: 4, core: 2. Of those that a mesh axis runs over, the one named last changes fastest.
Arguments:
- projections: float32 [16, 512, 4096], P(('groups', 'angle'), 'rows'), parts along dimension 0, may hold values from 0 to 6
- rowmap: int32 [16, 256], P(('groups', 'angle')), parts along dimension 0, may hold values from 0 to 511, as said below
- offsets: int32 [16, 8192], P(('groups', 'angle')), parts along dimension 0, may hold values from 0 to 4094
- fractions: float32 [16, 8192], P(('groups', 'angle')), parts along dimension 0, may hold values from 0 to 1
- distance_weight: float32 [16, 8192], P(('groups', 'angle')), parts along dimension 0, may hold values from 0.5 to 2
Outputs:
- volume: float32 [512, 8192], P(('groups', 'rows'), 'angle'), parts along dimension 0
The draws below stay inside these ranges and needn't reach their ends.
There are 2 independent parts, one for each index of `groups`. The reference program is written for one: setup_inputs(seed, part) draws one part's arguments, and reference() takes and returns one part's arrays. A program takes and returns all parts, laid end to end along the dimension named above; each array names one. Nothing has to cross between parts.
Inputs may be any that keep to these rules, and one draw needn't show every extreme that they name: `rowmap`: the plane stored at index k * 64 + m is the physical plane q = m * 4 + k, and in every projection it reads a row from 2 * q to 2 * q + 1.
All inputs are finite; a program needn't handle non-finite values.
Results may differ from the reference program's by a relative error of at most 0.0004.
The reference program's roundings to bfloat16 on the way (of `weighted`, `ramp`, `filtered` and `selected`) count: a program that leaves them out, or rounds other values in their place, can miss the bound.
Values may be sent and summed in bfloat16 or wider, within the bound.
A program may use at most 128 MiB of HBM per device.

```python
import math
import jax
import jax.numpy as jnp
from jax import lax

U = 4096
BAND = 128
ZDEV = 64
P_SIZE = 8
NV = 512
NZ = 256
NPIX = 8192


def draw_rowmap(key, part):
    key = jax.random.fold_in(key, 7)
    slabs = NZ // ZDEV
    stride_rows = BAND // ZDEV
    jitter = jax.random.randint(key, (P_SIZE, NZ), 0, stride_rows).astype(jnp.int32)
    jitter = jitter.at[0, 0].set(0)
    jitter = jitter.at[0, NZ - 1].set(stride_rows - 1)
    stored = jnp.arange(NZ, dtype=jnp.int32)
    slab = stored // ZDEV
    within = stored % ZDEV
    physical = within * slabs + slab
    rowlist = physical[None, :] * stride_rows + jitter
    return rowlist.astype(jnp.int32)


def chord_sum(column, height_pos, center_u, center_v, radius_u, radius_v, strength):
    summed = jnp.zeros((P_SIZE, NV, U), jnp.float32)
    for which in range(center_u.shape[1]):
        across = (column - center_u[:, which, None, None]) / radius_u[:, which, None, None]
        upward = (height_pos - center_v[:, which, None, None]) / radius_v[:, which, None, None]
        inside = jnp.maximum(1.0 - across * across - upward * upward, 0.0)
        summed = summed + strength[:, which, None, None] * jnp.sqrt(inside)
    return summed


def draw_projections(key, part):
    key = jax.random.fold_in(key, 11)
    parts_keys = jax.random.split(key, 6)
    column = ((jnp.arange(U, dtype=jnp.float32) + 0.5) / U)[None, None, :]
    height_pos = ((jnp.arange(NV, dtype=jnp.float32) + 0.5) / NV)[None, :, None]
    layout = (P_SIZE, 6)
    center_u = jax.random.uniform(parts_keys[0], layout, jnp.float32, 0.15, 0.85)
    center_v = jax.random.uniform(parts_keys[1], layout, jnp.float32, 0.15, 0.85)
    radius_u = jax.random.uniform(parts_keys[2], layout, jnp.float32, 0.15, 0.5)
    radius_v = jax.random.uniform(parts_keys[3], layout, jnp.float32, 0.2, 0.6)
    strength = jax.random.uniform(parts_keys[4], layout, jnp.float32, 0.3, 0.75)
    rough = jax.random.uniform(parts_keys[5], (P_SIZE, NV, U), jnp.float32, 0.0, 1.5)
    return chord_sum(column, height_pos, center_u, center_v, radius_u, radius_v, strength) + rough


def touch_ends(result, own_key, least, top_value):
    shape = result.shape
    spot = [jax.random.randint(jax.random.fold_in(own_key, axis), (), 0, shape[axis]) for axis in range(len(shape))]
    result = result.at[tuple(spot)].set(least)
    longest = shape.index(max(shape))
    spot[longest] = (spot[longest] + 1) % shape[longest]
    return result.at[tuple(spot)].set(top_value)


def block_levels(stream_key, extent, pieces, smallest, top_value):
    factor_of, own = 1.0, jax.random.fold_in(stream_key, 6)
    for axis_at, shards_of in pieces:
        heights = jnp.exp(jax.random.uniform(jax.random.fold_in(own, axis_at), (shards_of,), jnp.float32, smallest / len(pieces), top_value / len(pieces)))
        factor_of = factor_of * jnp.repeat(heights, extent[axis_at] // shards_of).reshape([-1 if axis == axis_at else 1 for axis in range(len(extent))])
    return factor_of


def setup_inputs(seed: int = 0, part: int = 0) -> dict:
    key_list = jax.random.split(jax.random.key(seed), 6)
    own_keys = jax.random.split(jax.random.fold_in(key_list[5], part), 6)
    return {
        "projections": draw_projections(jax.random.fold_in(jax.random.fold_in(key_list[5], part), 71), part),
        "rowmap": draw_rowmap(jax.random.fold_in(jax.random.fold_in(key_list[5], part), 71), part),
        "offsets": touch_ends(jax.random.randint(own_keys[2], (P_SIZE, NPIX), 0, U - 1), jax.random.fold_in(own_keys[2], 1), 0, (U - 1) - 1).astype(jnp.int32),
        "fractions": jnp.clip(1.0 * jax.random.uniform(own_keys[3], (P_SIZE, NPIX), jnp.float32) ** block_levels(own_keys[3], (P_SIZE, NPIX), ((0, 4),), -0.2, 0.2), 0.0, 1.0),
        "distance_weight": jnp.clip(jnp.exp(math.log(2.0) - 1.3862944 * jax.random.uniform(own_keys[4], (P_SIZE, NPIX), jnp.float32) ** block_levels(own_keys[4], (P_SIZE, NPIX), ((0, 4),), -0.2, 0.2)), 0.5, 2.0),
    }


def ramp_table(offset):
    magnitude = jnp.abs(offset)
    spread = jnp.maximum(magnitude, 1).astype(jnp.float32)
    odd_term = -1.0 / (math.pi ** 2 * spread * spread)
    value = jnp.where(magnitude == 0, 0.25, jnp.where(magnitude % 2 == 1, odd_term, 0.0))
    return value.astype(jnp.bfloat16)

def cone_weight(row_value, width, height):
    column = jnp.arange(width, dtype=jnp.float32) - (width - 1) / 2.0
    vertical = row_value - (height - 1) / 2.0
    distance = 2.0 * width
    return distance / jnp.sqrt(distance * distance + column * column + vertical * vertical)

def reference(projections, rowmap, offsets, fractions, distance_weight):
    rows = jax.vmap(lambda plane_set, index: jnp.take(plane_set, index, axis=0))(projections, rowmap)
    row_value = rowmap.astype(jnp.float32)[:, :, None]
    weighted = (rows * cone_weight(row_value, U, NV)).astype(jnp.bfloat16)
    source = lax.broadcasted_iota(jnp.int32, (U, U), 0)
    target = lax.broadcasted_iota(jnp.int32, (U, U), 1)
    ramp = ramp_table(target - source)
    flat = weighted.reshape(P_SIZE * NZ, U)
    filtered = jnp.dot(flat, ramp, preferred_element_type=jnp.float32).astype(jnp.bfloat16).reshape(P_SIZE, NZ, U)

    def add_view(total, items):
        selected, offset, fraction, weight = items
        lower = jnp.take(selected, offset, axis=1).astype(jnp.float32)
        upper = jnp.take(selected, offset + 1, axis=1).astype(jnp.float32)
        near_weight = weight * (1.0 - fraction)
        far_weight = weight * fraction
        return (total + near_weight[None, :] * lower + far_weight[None, :] * upper, None)
    volume, _ = lax.scan(add_view, jnp.zeros((NZ, NPIX), jnp.float32), (filtered, offsets, fractions, distance_weight))
    return volume
```

```python
import functools
import math

import jax
import jax.numpy as jnp
import ml_dtypes
import numpy as np
from jax import lax
from jax.experimental import pallas as pl
from jax.experimental.pallas import tpu as pltpu
from jax.sharding import PartitionSpec as P

BLOCK = 256
PIX = 128
GROUP = 32
MESH = pl.DeviceIdType.MESH


def ramp_values(lag):
    magnitude = np.abs(lag)
    spread = np.maximum(magnitude, 1).astype(np.float32)
    odd_term = np.float32(-1.0) / (np.float32(math.pi**2) * spread * spread)
    value = np.where(magnitude % 2 == 1, odd_term, np.float32(0.0))
    return value.astype(ml_dtypes.bfloat16)


def odd_lag_tables(width):
    half = width // 2
    blocks = half // BLOCK
    row = np.arange(BLOCK)[:, None]
    column = np.arange((2 * blocks - 1) * BLOCK)[None, :] - (blocks - 1) * BLOCK
    difference = row - column
    return np.stack([ramp_values(2 * difference - 1), ramp_values(2 * difference + 1)])


def kernel(
    dims,
    x_ref,
    chosen_ref,
    ramp_ref,
    idx_mine,
    idx_theirs,
    wgt_mine,
    wgt_theirs,
    out_ref,
    xt,
    te,
    to,
    tables,
    idx_smem,
    idx_recv,
    wgt_recv,
    rows_buf,
    stage,
    arrived,
    zstage,
    x_send,
    x_recv,
    idx_sems,
    part_send,
    part_recv,
    z_send,
    z_recv,
    smem_sems,
):
    angles, bands, band, width, zdev, npq, chunk = dims
    pairs = angles // 2
    capacity = zdev // bands
    chunks = npq // chunk
    half = width // 2
    height = band * bands
    rows2 = 2 * zdev
    me = lax.axis_index("angle")
    here = lax.axis_index("rows")
    my_pair = me // 2
    parity = me - 2 * my_pair
    partner = {"angle": 2 * my_pair + 1 - parity}

    def pair_peer(step):
        return lax.rem(my_pair + step, pairs)

    def band_peer(step):
        return lax.rem(here + step, bands)

    own_idx = pltpu.make_async_copy(
        idx_mine, idx_smem.at[pl.ds(0, 2 * pairs * npq)], smem_sems.at[0]
    )
    own_idx.start()

    barrier = pltpu.get_barrier_semaphore()
    pl.semaphore_signal(barrier, inc=1, device_id=partner, device_id_type=MESH)
    for step in range(1, pairs):
        pl.semaphore_signal(
            barrier,
            inc=1,
            device_id={"angle": 2 * pair_peer(step) + parity},
            device_id_type=MESH,
        )
    for step in range(1, bands):
        pl.semaphore_signal(
            barrier, inc=1, device_id={"rows": band_peer(step)}, device_id_type=MESH
        )
    pl.semaphore_wait(barrier, pairs + bands - 1)

    send_idx = pltpu.make_async_remote_copy(
        idx_theirs, idx_recv, idx_sems.at[0], idx_sems.at[1], device_id=partner, device_id_type=MESH
    )
    send_idx.start()
    send_wgt = pltpu.make_async_remote_copy(
        wgt_theirs, wgt_recv, idx_sems.at[2], idx_sems.at[3], device_id=partner, device_id_type=MESH
    )
    send_wgt.start()

    lane_row = lax.broadcasted_iota(jnp.int32, (zdev, band), 1)
    select = [
        (chosen_ref[p * zdev : (p + 1) * zdev, :] == lane_row).astype(jnp.bfloat16)
        for p in range(2)
    ]
    target = lax.broadcasted_iota(jnp.int32, (BLOCK, BLOCK), 0)
    source = lax.broadcasted_iota(jnp.int32, (BLOCK, BLOCK), 1)
    wanted = jnp.where(target < BLOCK // 2, 2 * target, 2 * target - BLOCK + 1)
    unshuffle = (wanted == source).astype(jnp.bfloat16)
    row_value = (here * band + lax.broadcasted_iota(jnp.int32, (band, 1), 0)).astype(jnp.float32)
    vertical = row_value - (height - 1) / 2.0
    vertical_square = vertical * vertical
    distance = 2.0 * width

    for block in range(width // BLOCK):
        first = block * BLOCK
        column = lax.broadcasted_iota(jnp.int32, (1, BLOCK), 1).astype(jnp.float32) + (
            first - (width - 1) / 2.0
        )
        cosine = distance / jnp.sqrt(distance * distance + column * column + vertical_square)
        picked = []
        for p in range(2):
            weighted = (x_ref[p, :, first : first + BLOCK] * cosine).astype(jnp.bfloat16)
            picked.append(jnp.dot(select[p], weighted, preferred_element_type=jnp.float32))
        picked = jnp.concatenate(picked, axis=0).astype(jnp.bfloat16)
        turned = lax.dot_general(
            unshuffle, picked, (((1,), (1,)), ((), ())), preferred_element_type=jnp.float32
        ).astype(jnp.bfloat16)
        at = block * (BLOCK // 2)
        xt[0, at : at + BLOCK // 2, 0:rows2] = turned[: BLOCK // 2]
        xt[1, at : at + BLOCK // 2, 0:rows2] = turned[BLOCK // 2 :]

    send_x = pltpu.make_async_remote_copy(
        xt.at[:, :, pl.ds(0, rows2)],
        xt.at[:, :, pl.ds(rows2, rows2)],
        x_send,
        x_recv,
        device_id=partner,
        device_id_type=MESH,
    )
    send_x.start()

    send_idx.wait_recv()
    other_idx = pltpu.make_async_copy(
        idx_recv, idx_smem.at[pl.ds(2 * pairs * npq, 2 * pairs * npq)], smem_sems.at[1]
    )
    other_idx.start()

    send_x.wait()

    blocks = half // BLOCK
    for block in range(blocks):
        start = (blocks - 1 - block) * BLOCK
        at = block * BLOCK
        for side, out in ((0, te), (1, to)):
            total = jnp.dot(
                ramp_ref[side, :, start : start + half],
                xt[1 - side],
                preferred_element_type=jnp.float32,
            )
            total = total + 0.25 * xt[side, at : at + BLOCK, :].astype(jnp.float32)
            out[at : at + BLOCK, :] = total.astype(jnp.bfloat16).astype(jnp.float32)
    te[half : half + 8, :] = jnp.zeros((8, 2 * rows2), jnp.float32)

    low = lax.broadcasted_iota(jnp.int32, (BLOCK, rows2), 1) < zdev

    def build(block, carry):
        at = pl.multiple_of(block * BLOCK, BLOCK)
        for side in range(2):
            lanes = slice(side * rows2, (side + 1) * rows2)
            even = te[pl.ds(at, BLOCK), lanes]
            odd = to[pl.ds(at, BLOCK), lanes]
            later = te[pl.ds(at, BLOCK + 8), lanes][1 : BLOCK + 1]
            turned_odd = pltpu.roll(odd, zdev, 1)
            tables[2 * side, pl.ds(at, BLOCK), :] = jnp.where(low, even, turned_odd)
            tables[2 * side + 1, pl.ds(at, BLOCK), :] = jnp.where(
                low, pltpu.roll(even, zdev, 1), odd
            )
            tables[2 * side, pl.ds(half + at, BLOCK), :] = jnp.where(
                low, odd, pltpu.roll(later, zdev, 1)
            )
            tables[2 * side + 1, pl.ds(half + at, BLOCK), :] = jnp.where(low, turned_odd, later)
        return carry

    lax.fori_loop(0, blocks, build, 0)

    own_idx.wait()
    other_idx.wait()
    send_wgt.wait_recv()

    def gather(quarter, first):
        base = quarter * npq + first

        def rows(group, carry):
            at = pl.multiple_of(group * GROUP, GROUP)
            for r in range(GROUP):
                for q in range(4):
                    index = idx_smem[q * pairs * npq + base + at + r]
                    rows_buf[q, pl.ds(at + r, 1), :] = tables[q, pl.ds(index, 1), :]
            return carry

        lax.fori_loop(0, PIX // GROUP, rows, 0)
        total = None
        for q in range(4):
            turned = rows_buf[q].T
            weights = wgt_mine if q < 2 else wgt_recv
            spot = pl.ds(pl.multiple_of(base, PIX), PIX)
            near = weights[pl.ds(2 * (q % 2), 1), spot]
            far = weights[pl.ds(2 * (q % 2) + 1, 1), spot]
            term = near * turned[:zdev] + far * turned[zdev:]
            total = term if total is None else total + term
        return total

    def part_copy(step, piece):
        return pltpu.make_async_remote_copy(
            stage.at[step - 1, piece],
            arrived.at[step - 1, piece],
            part_send.at[step - 1, piece],
            part_recv.at[step - 1, piece],
            device_id={"angle": 2 * pair_peer(step) + parity},
            device_id_type=MESH,
        )

    def z_copy(step, piece):
        return pltpu.make_async_remote_copy(
            zstage.at[piece, band_peer(step)],
            out_ref.at[here, :, pl.ds(pl.multiple_of(piece * chunk, chunk), chunk)],
            z_send.at[step - 1, piece],
            z_recv.at[step - 1, piece],
            device_id={"rows": band_peer(step)},
            device_id_type=MESH,
        )

    for step in range(1, pairs):

        def others(piece, carry):
            def one(part, carry):
                at = pl.multiple_of(part * PIX, PIX)
                stage[step - 1, piece, :, pl.ds(at, PIX)] = gather(
                    pair_peer(step), piece * chunk + at
                )
                return carry

            lax.fori_loop(0, chunk // PIX, one, 0)
            part_copy(step, piece).start()
            return carry

        lax.fori_loop(0, chunks, others, 0)

    def own(piece, carry):
        for step in range(1, pairs):
            part_copy(step, piece).wait_recv()

        def one(part, carry):
            at = pl.multiple_of(part * PIX, PIX)
            total = gather(my_pair, piece * chunk + at)
            for step in range(1, pairs):
                total = total + arrived[step - 1, piece, :, pl.ds(at, PIX)]
            for b in range(bands):
                zstage[piece, b, :, pl.ds(at, PIX)] = total[b * capacity : (b + 1) * capacity]
            return carry

        lax.fori_loop(0, chunk // PIX, one, 0)
        for step in range(1, bands):
            z_copy(step, piece).start()
        spot = pl.ds(pl.multiple_of(piece * chunk, chunk), chunk)
        out_ref[here, :, spot] = zstage[piece, here]
        return carry

    lax.fori_loop(0, chunks, own, 0)

    send_idx.wait_send()
    send_wgt.wait_send()

    def drain(piece, carry):
        for step in range(1, pairs):
            part_copy(step, piece).wait_send()
        for step in range(1, bands):
            z_copy(step, piece).wait()
        return carry

    lax.fori_loop(0, chunks, drain, 0)


def local(projections, rowmap, offsets, fractions, distance_weight):
    bands = lax.axis_size("rows")
    angles = lax.axis_size("angle")
    here = lax.axis_index("rows")
    parity = lax.rem(lax.axis_index("angle"), 2)
    _, band, width = projections.shape
    zdev = rowmap.shape[1] // bands
    capacity = zdev // bands
    pixels = offsets.shape[1]
    npq = pixels // angles
    pairs = angles // 2
    chunk = min(512, npq)
    chunks = npq // chunk
    half = width // 2

    chosen = lax.dynamic_slice_in_dim(
        rowmap.reshape(2, bands, zdev), here * capacity, capacity, 2
    ).reshape(2 * zdev, 1) - here * band

    index = (offsets % 2) * half + offsets // 2
    index = index.reshape(2, pairs, 2, npq)
    weights = jnp.stack(
        [distance_weight * (1.0 - fractions), distance_weight * fractions], axis=1
    ).reshape(4, pairs, 2, npq)

    def of_parity(array, which):
        return lax.dynamic_index_in_dim(array, which, 2, keepdims=False)

    idx_mine = of_parity(index, parity).reshape(-1)
    idx_theirs = of_parity(index, 1 - parity).reshape(-1)
    wgt_mine = of_parity(weights, parity).reshape(4, pairs * npq)
    wgt_theirs = of_parity(weights, 1 - parity).reshape(4, pairs * npq)
    ramp = jnp.asarray(odd_lag_tables(width))

    dims = (angles, bands, band, width, zdev, npq, chunk)
    vmem = pl.BlockSpec(memory_space=pltpu.VMEM)
    rows2 = 2 * zdev
    peers = max(pairs - 1, 1)
    out = pl.pallas_call(
        functools.partial(kernel, dims),
        out_shape=jax.ShapeDtypeStruct((bands, capacity, npq), jnp.float32),
        in_specs=[vmem] * 7,
        out_specs=vmem,
        scratch_shapes=[
            pltpu.VMEM((2, half, 2 * rows2), jnp.bfloat16),
            pltpu.VMEM((half + 8, 2 * rows2), jnp.float32),
            pltpu.VMEM((half, 2 * rows2), jnp.float32),
            pltpu.VMEM((4, width, rows2), jnp.float32),
            pltpu.SMEM((4 * pairs * npq,), jnp.int32),
            pltpu.VMEM((2 * pairs * npq,), jnp.int32),
            pltpu.VMEM((4, pairs * npq), jnp.float32),
            pltpu.VMEM((4, PIX, rows2), jnp.float32),
            pltpu.VMEM((peers, chunks, zdev, chunk), jnp.float32),
            pltpu.VMEM((peers, chunks, zdev, chunk), jnp.float32),
            pltpu.VMEM((chunks, bands, capacity, chunk), jnp.float32),
            pltpu.SemaphoreType.DMA,
            pltpu.SemaphoreType.DMA,
            pltpu.SemaphoreType.DMA((4,)),
            pltpu.SemaphoreType.DMA((peers, chunks)),
            pltpu.SemaphoreType.DMA((peers, chunks)),
            pltpu.SemaphoreType.DMA((max(bands - 1, 1), chunks)),
            pltpu.SemaphoreType.DMA((max(bands - 1, 1), chunks)),
            pltpu.SemaphoreType.DMA((2,)),
        ],
        compiler_params=pltpu.CompilerParams(
            collective_id=0, has_side_effects=True, vmem_limit_bytes=56 * 1024 * 1024
        ),
    )(projections, chosen, ramp, idx_mine, idx_theirs, wgt_mine, wgt_theirs)
    return out.reshape(zdev, npq)


def solution(mesh):
    in_specs = (
        P(("groups", "angle"), "rows", None),
        P(("groups", "angle"), None),
        P(("groups", "angle"), None),
        P(("groups", "angle"), None),
        P(("groups", "angle"), None),
    )
    out_specs = P(("groups", "rows"), "angle")
    return jax.shard_map(local, mesh=mesh, in_specs=in_specs, out_specs=out_specs, check_vma=False)
```

```python
import functools
import math

import jax
import jax.numpy as jnp
import ml_dtypes
import numpy as np
from jax import lax
from jax.experimental import pallas as pl
from jax.experimental.pallas import tpu as pltpu
from jax.sharding import PartitionSpec as P

BLOCK = 256
PIX = 128
GROUP = 32
MESH = pl.DeviceIdType.MESH


def ramp_values(lag):
    magnitude = np.abs(lag)
    spread = np.maximum(magnitude, 1).astype(np.float32)
    odd_term = np.float32(-1.0) / (np.float32(math.pi**2) * spread * spread)
    value = np.where(magnitude % 2 == 1, odd_term, np.float32(0.0))
    return value.astype(ml_dtypes.bfloat16)


def odd_lag_tables(width):
    half = width // 2
    blocks = half // BLOCK
    row = np.arange(BLOCK)[:, None]
    column = np.arange((2 * blocks - 1) * BLOCK)[None, :] - (blocks - 1) * BLOCK
    difference = row - column
    return np.stack([ramp_values(2 * difference - 1), ramp_values(2 * difference + 1)])


def kernel(
    dims,
    x_hbm,
    rowmap_ref,
    offsets_hbm,
    fractions_hbm,
    weight_hbm,
    ramp_hbm,
    out_ref,
    x_buf,
    ramp_buf,
    off_own,
    off_other,
    off_recv,
    frac_own,
    frac_other,
    dist_own,
    dist_other,
    onehot,
    select,
    xt,
    te,
    to,
    tables,
    rows_buf,
    mine,
    stage,
    arrived,
    zstage,
    x_sems,
    in_sems,
    small_sems,
    xt_send,
    xt_recv,
    part_send,
    part_recv,
    z_send,
    z_recv,
):
    angles, bands, band, width, zdev, npq, chunk = dims
    pairs = angles // 2
    capacity = zdev // bands
    chunks = npq // chunk
    half = width // 2
    height = band * bands
    rows2 = 2 * zdev
    slices = 4
    columns = width // slices
    me = lax.axis_index("angle")
    here = lax.axis_index("rows")
    my_pair = me // 2
    parity = me - 2 * my_pair
    partner = {"angle": 2 * my_pair + 1 - parity}

    def pair_peer(step):
        return lax.rem(my_pair + step, pairs)

    def band_peer(step):
        return lax.rem(here + step, bands)

    barrier = pltpu.get_barrier_semaphore()
    pl.semaphore_signal(barrier, inc=1, device_id=partner, device_id_type=MESH)
    for step in range(1, pairs):
        pl.semaphore_signal(
            barrier,
            inc=1,
            device_id={"angle": 2 * pair_peer(step) + parity},
            device_id_type=MESH,
        )
    for step in range(1, bands):
        pl.semaphore_signal(
            barrier, inc=1, device_id={"rows": band_peer(step)}, device_id_type=MESH
        )

    def x_copy(part):
        spot = pl.ds(part * columns, columns)
        return pltpu.make_async_copy(
            x_hbm.at[:, :, spot], x_buf.at[:, :, spot], x_sems.at[part]
        )

    for part in range(slices):
        x_copy(part).start()
    inputs = [
        pltpu.make_async_copy(ramp_hbm, ramp_buf, in_sems.at[0]),
        pltpu.make_async_copy(offsets_hbm, off_own, in_sems.at[1]),
        pltpu.make_async_copy(fractions_hbm, frac_own, in_sems.at[2]),
        pltpu.make_async_copy(weight_hbm, dist_own, in_sems.at[3]),
    ]
    for copy in inputs:
        copy.start()

    row_of = lax.broadcasted_iota(jnp.int32, (band, rowmap_ref.shape[1]), 0) + here * band
    for p in range(2):
        hit = (rowmap_ref[p : p + 1, :] == row_of).astype(jnp.float32)
        onehot[p] = hit.T
        for slab in range(bands):
            for m in range(capacity):
                spot = slab * capacity + m
                select[p, spot : spot + 1, :] = onehot[
                    p, pl.ds(slab * zdev + here * capacity + m, 1), :
                ]
    chosen = [select[p].astype(jnp.bfloat16) for p in range(2)]

    pl.semaphore_wait(barrier, pairs + bands - 1)

    def to_partner(src, dst, at):
        return pltpu.make_async_remote_copy(
            src,
            dst,
            small_sems.at[0, at],
            small_sems.at[1, at],
            device_id=partner,
            device_id_type=MESH,
        )

    small = [
        to_partner(offsets_hbm, off_recv, 0),
        to_partner(fractions_hbm, frac_other, 1),
        to_partner(weight_hbm, dist_other, 2),
    ]
    for copy in small:
        copy.start()

    target = lax.broadcasted_iota(jnp.int32, (BLOCK, BLOCK), 0)
    source = lax.broadcasted_iota(jnp.int32, (BLOCK, BLOCK), 1)
    wanted = jnp.where(target < BLOCK // 2, 2 * target, 2 * target - BLOCK + 1)
    unshuffle = (wanted == source).astype(jnp.bfloat16)
    row_value = (here * band + lax.broadcasted_iota(jnp.int32, (band, 1), 0)).astype(jnp.float32)
    vertical = row_value - (height - 1) / 2.0
    vertical_square = vertical * vertical
    distance = 2.0 * width

    def xt_copy(part):
        spot = pl.ds(part * (columns // 2), columns // 2)
        return pltpu.make_async_remote_copy(
            xt.at[:, spot, pl.ds(0, rows2)],
            xt.at[:, spot, pl.ds(rows2, rows2)],
            xt_send.at[part],
            xt_recv.at[part],
            device_id=partner,
            device_id_type=MESH,
        )

    for part in range(slices):
        x_copy(part).wait()
        for block in range(part * columns // BLOCK, (part + 1) * columns // BLOCK):
            first = block * BLOCK
            column = lax.broadcasted_iota(jnp.int32, (1, BLOCK), 1).astype(jnp.float32) + (
                first - (width - 1) / 2.0
            )
            cosine = distance / jnp.sqrt(distance * distance + column * column + vertical_square)
            picked = []
            for p in range(2):
                weighted = (x_buf[p, :, first : first + BLOCK] * cosine).astype(jnp.bfloat16)
                picked.append(jnp.dot(chosen[p], weighted, preferred_element_type=jnp.float32))
            picked = jnp.concatenate(picked, axis=0).astype(jnp.bfloat16)
            turned = lax.dot_general(
                unshuffle, picked, (((1,), (1,)), ((), ())), preferred_element_type=jnp.float32
            ).astype(jnp.bfloat16)
            at = block * (BLOCK // 2)
            xt[0, at : at + BLOCK // 2, 0:rows2] = turned[: BLOCK // 2]
            xt[1, at : at + BLOCK // 2, 0:rows2] = turned[BLOCK // 2 :]
        xt_copy(part).start()

    small[0].wait_recv()
    last_input = pltpu.make_async_copy(off_recv, off_other, in_sems.at[4])
    last_input.start()
    inputs[0].wait()
    for part in range(slices):
        xt_copy(part).wait_recv()

    low = lax.broadcasted_iota(jnp.int32, (BLOCK, rows2), 1) < zdev
    te[half : half + 8, :] = jnp.zeros((8, 2 * rows2), jnp.float32)
    blocks = half // BLOCK
    for block in reversed(range(blocks)):
        start = (blocks - 1 - block) * BLOCK
        at = block * BLOCK
        for side, out in ((0, te), (1, to)):
            total = jnp.dot(
                ramp_buf[side, :, start : start + half],
                xt[1 - side],
                preferred_element_type=jnp.float32,
            )
            total = total + 0.25 * xt[side, at : at + BLOCK, :].astype(jnp.float32)
            out[at : at + BLOCK, :] = total.astype(jnp.bfloat16).astype(jnp.float32)
        for side in range(2):
            lanes = slice(side * rows2, (side + 1) * rows2)
            even = te[at : at + BLOCK, lanes]
            odd = to[at : at + BLOCK, lanes]
            later = te[at + 1 : at + 1 + BLOCK, lanes]
            turned_odd = pltpu.roll(odd, zdev, 1)
            evens = pl.ds(2 * at, BLOCK, stride=2)
            odds = pl.ds(2 * at + 1, BLOCK, stride=2)
            tables[2 * side, evens, :] = jnp.where(low, even, turned_odd)
            tables[2 * side + 1, evens, :] = jnp.where(low, pltpu.roll(even, zdev, 1), odd)
            tables[2 * side, odds, :] = jnp.where(low, odd, pltpu.roll(later, zdev, 1))
            tables[2 * side + 1, odds, :] = jnp.where(low, turned_odd, later)

    for copy in inputs[1:] + [last_input]:
        copy.wait()
    for copy in small[1:]:
        copy.wait_recv()

    def gather(pair, first):
        base = (2 * pair + parity) * npq + first

        def rows(group, carry):
            at = pl.multiple_of(group * GROUP, GROUP)
            for r in range(GROUP):
                for q in range(4):
                    offsets = off_own if q < 2 else off_other
                    index = offsets[q % 2, base + at + r]
                    rows_buf[q, pl.ds(at + r, 1), :] = tables[q, pl.ds(index, 1), :]
            return carry

        lax.fori_loop(0, PIX // GROUP, rows, 0)
        total = None
        spot = pl.ds(pl.multiple_of(base, PIX), PIX)
        for q in range(4):
            turned = rows_buf[q].T
            fractions = (frac_own if q < 2 else frac_other)[pl.ds(q % 2, 1), spot]
            weight = (dist_own if q < 2 else dist_other)[pl.ds(q % 2, 1), spot]
            near = weight * (1.0 - fractions)
            far = weight * fractions
            term = near * turned[:zdev] + far * turned[zdev:]
            total = term if total is None else total + term
        return total

    def part_copy(step, piece):
        return pltpu.make_async_remote_copy(
            stage.at[step - 1, piece],
            arrived.at[step - 1, piece],
            part_send.at[step - 1, piece],
            part_recv.at[step - 1, piece],
            device_id={"angle": 2 * pair_peer(step) + parity},
            device_id_type=MESH,
        )

    def z_copy(step, piece):
        return pltpu.make_async_remote_copy(
            zstage.at[piece, band_peer(step)],
            out_ref.at[here, :, pl.ds(pl.multiple_of(piece * chunk, chunk), chunk)],
            z_send.at[step - 1, piece],
            z_recv.at[step - 1, piece],
            device_id={"rows": band_peer(step)},
            device_id_type=MESH,
        )

    for step in range(1, pairs):

        def others(piece, carry):
            for part in range(chunk // PIX):
                at = part * PIX
                stage[step - 1, piece, :, at : at + PIX] = gather(
                    pair_peer(step), piece * chunk + at
                )
            part_copy(step, piece).start()
            return carry

        lax.fori_loop(0, chunks, others, 0)

    def own(piece, carry):
        for part in range(chunk // PIX):
            at = part * PIX
            mine[piece, :, at : at + PIX] = gather(my_pair, piece * chunk + at)
        return carry

    lax.fori_loop(0, chunks, own, 0)

    def combine(piece, carry):
        total = mine[piece]
        for step in range(1, pairs):
            part_copy(step, piece).wait_recv()
            total = total + arrived[step - 1, piece]
        for b in range(bands):
            zstage[piece, b] = total[b * capacity : (b + 1) * capacity]
        for step in range(1, bands):
            z_copy(step, piece).start()
        spot = pl.ds(pl.multiple_of(piece * chunk, chunk), chunk)
        out_ref[here, :, spot] = zstage[piece, here]
        return carry

    lax.fori_loop(0, chunks, combine, 0)

    for copy in small:
        copy.wait_send()
    for part in range(slices):
        xt_copy(part).wait_send()

    def drain(piece, carry):
        for step in range(1, pairs):
            part_copy(step, piece).wait_send()
        for step in range(1, bands):
            z_copy(step, piece).wait()
        return carry

    lax.fori_loop(0, chunks, drain, 0)


def local(projections, rowmap, offsets, fractions, distance_weight):
    bands = lax.axis_size("rows")
    angles = lax.axis_size("angle")
    _, band, width = projections.shape
    planes = rowmap.shape[1]
    zdev = planes // bands
    capacity = zdev // bands
    pixels = offsets.shape[1]
    npq = pixels // angles
    pairs = angles // 2
    chunk = min(256, npq)
    chunks = npq // chunk
    half = width // 2
    ramp = jnp.asarray(odd_lag_tables(width))

    dims = (angles, bands, band, width, zdev, npq, chunk)
    vmem = pl.BlockSpec(memory_space=pltpu.VMEM)
    hbm = pl.BlockSpec(memory_space=pl.ANY)
    rows2 = 2 * zdev
    peers = max(pairs - 1, 1)
    small = pltpu.VMEM((2, pixels), jnp.float32)
    out = pl.pallas_call(
        functools.partial(kernel, dims),
        out_shape=jax.ShapeDtypeStruct((bands, capacity, npq), jnp.float32),
        in_specs=[hbm, vmem, hbm, hbm, hbm, hbm],
        out_specs=vmem,
        scratch_shapes=[
            pltpu.VMEM((2, band, width), jnp.float32),
            pltpu.VMEM(ramp.shape, jnp.bfloat16),
            pltpu.SMEM((2, pixels), jnp.int32),
            pltpu.SMEM((2, pixels), jnp.int32),
            pltpu.VMEM((2, pixels), jnp.int32),
            small,
            small,
            small,
            small,
            pltpu.VMEM((2, planes, band), jnp.float32),
            pltpu.VMEM((2, zdev, band), jnp.float32),
            pltpu.VMEM((2, half, 2 * rows2), jnp.bfloat16),
            pltpu.VMEM((half + 8, 2 * rows2), jnp.float32),
            pltpu.VMEM((half, 2 * rows2), jnp.float32),
            pltpu.VMEM((4, width, rows2), jnp.float32),
            pltpu.VMEM((4, PIX, rows2), jnp.float32),
            pltpu.VMEM((chunks, zdev, chunk), jnp.float32),
            pltpu.VMEM((peers, chunks, zdev, chunk), jnp.float32),
            pltpu.VMEM((peers, chunks, zdev, chunk), jnp.float32),
            pltpu.VMEM((chunks, bands, capacity, chunk), jnp.float32),
            pltpu.SemaphoreType.DMA((4,)),
            pltpu.SemaphoreType.DMA((5,)),
            pltpu.SemaphoreType.DMA((2, 3)),
            pltpu.SemaphoreType.DMA((4,)),
            pltpu.SemaphoreType.DMA((4,)),
            pltpu.SemaphoreType.DMA((peers, chunks)),
            pltpu.SemaphoreType.DMA((peers, chunks)),
            pltpu.SemaphoreType.DMA((max(bands - 1, 1), chunks)),
            pltpu.SemaphoreType.DMA((max(bands - 1, 1), chunks)),
        ],
        compiler_params=pltpu.CompilerParams(
            collective_id=0, has_side_effects=True, vmem_limit_bytes=56 * 1024 * 1024
        ),
    )(projections, rowmap, offsets, fractions, distance_weight, ramp)
    return out.reshape(zdev, npq)


def solution(mesh):
    in_specs = (
        P(("groups", "angle"), "rows", None),
        P(("groups", "angle"), None),
        P(("groups", "angle"), None),
        P(("groups", "angle"), None),
        P(("groups", "angle"), None),
    )
    out_specs = P(("groups", "rows"), "angle")
    return jax.shard_map(local, mesh=mesh, in_specs=in_specs, out_specs=out_specs, check_vma=False)
```

```python
import functools
import math

import jax
import jax.numpy as jnp
import ml_dtypes
import numpy as np
from jax import lax
from jax.experimental import pallas as pl
from jax.experimental.pallas import tpu as pltpu
from jax.sharding import PartitionSpec as P

BLOCK = 256
PIX = 128
GROUP = 32
LEAD = 2
MESH = pl.DeviceIdType.MESH


def ramp_values(lag):
    magnitude = np.abs(lag)
    spread = np.maximum(magnitude, 1).astype(np.float32)
    odd_term = np.float32(-1.0) / (np.float32(math.pi**2) * spread * spread)
    value = np.where(magnitude % 2 == 1, odd_term, np.float32(0.0))
    return value.astype(ml_dtypes.bfloat16)


def odd_lag_tables(width):
    half = width // 2
    blocks = half // BLOCK
    row = np.arange(BLOCK)[:, None]
    column = np.arange((2 * blocks - 1) * BLOCK)[None, :] - (blocks - 1) * BLOCK
    difference = row - column
    return np.stack([ramp_values(2 * difference - 1), ramp_values(2 * difference + 1)])


def kernel(
    dims,
    x_hbm,
    rowmap_ref,
    offsets_hbm,
    fractions_hbm,
    weight_hbm,
    ramp_hbm,
    out_ref,
    x_buf,
    ramp_buf,
    off_own,
    off_other,
    off_flat,
    off_recv,
    off_raw,
    frac_own,
    frac_other,
    dist_own,
    dist_other,
    onehot,
    select,
    xt,
    te,
    to,
    tables,
    rows_buf,
    mine,
    stage,
    arrived,
    zstage,
    x_sems,
    in_sems,
    small_sems,
    xt_send,
    xt_recv,
    part_send,
    part_recv,
    z_send,
    z_recv,
):
    angles, bands, band, width, zdev, npq, chunk = dims
    pairs = angles // 2
    capacity = zdev // bands
    chunks = npq // chunk
    half = width // 2
    height = band * bands
    rows2 = 2 * zdev
    slices = 4
    columns = width // slices
    me = lax.axis_index("angle")
    here = lax.axis_index("rows")
    my_pair = me // 2
    parity = me - 2 * my_pair
    partner = {"angle": 2 * my_pair + 1 - parity}

    def pair_peer(step):
        return lax.rem(my_pair + step, pairs)

    def band_peer(step):
        return lax.rem(here + step, bands)

    barrier = pltpu.get_barrier_semaphore()
    pl.semaphore_signal(barrier, inc=1, device_id=partner, device_id_type=MESH)
    for step in range(1, pairs):
        pl.semaphore_signal(
            barrier,
            inc=1,
            device_id={"angle": 2 * pair_peer(step) + parity},
            device_id_type=MESH,
        )
    for step in range(1, bands):
        pl.semaphore_signal(
            barrier, inc=1, device_id={"rows": band_peer(step)}, device_id_type=MESH
        )

    def x_copy(part):
        spot = pl.ds(part * columns, columns)
        return pltpu.make_async_copy(
            x_hbm.at[:, :, spot], x_buf.at[:, :, spot], x_sems.at[part]
        )

    for part in range(slices):
        x_copy(part).start()
    inputs = [
        pltpu.make_async_copy(ramp_hbm, ramp_buf, in_sems.at[0]),
        pltpu.make_async_copy(offsets_hbm, off_raw, in_sems.at[1]),
        pltpu.make_async_copy(fractions_hbm, frac_own, in_sems.at[2]),
        pltpu.make_async_copy(weight_hbm, dist_own, in_sems.at[3]),
    ]
    for copy in inputs:
        copy.start()

    row_of = lax.broadcasted_iota(jnp.int32, (band, rowmap_ref.shape[1]), 0) + here * band
    for p in range(2):
        hit = (rowmap_ref[p : p + 1, :] == row_of).astype(jnp.float32)
        onehot[p] = hit.T
        for slab in range(bands):
            for m in range(capacity):
                spot = slab * capacity + m
                select[p, spot : spot + 1, :] = onehot[
                    p, pl.ds(slab * zdev + here * capacity + m, 1), :
                ]
    chosen = [select[p].astype(jnp.bfloat16) for p in range(2)]

    inputs[1].wait()
    pixels = off_raw.shape[1]
    for p in range(2):
        raw = off_raw[p, :]
        off_flat[pl.ds(p * pixels, pixels)] = (raw & 1) * half + (raw >> 1)
    own_offsets = pltpu.make_async_copy(off_flat, off_own, in_sems.at[5])
    own_offsets.start()

    pl.semaphore_wait(barrier, pairs + bands - 1)

    def to_partner(src, dst, at):
        return pltpu.make_async_remote_copy(
            src,
            dst,
            small_sems.at[0, at],
            small_sems.at[1, at],
            device_id=partner,
            device_id_type=MESH,
        )

    small = [
        to_partner(off_flat, off_recv, 0),
        to_partner(fractions_hbm, frac_other, 1),
        to_partner(weight_hbm, dist_other, 2),
    ]
    for copy in small:
        copy.start()

    target = lax.broadcasted_iota(jnp.int32, (BLOCK, BLOCK), 0)
    source = lax.broadcasted_iota(jnp.int32, (BLOCK, BLOCK), 1)
    wanted = jnp.where(target < BLOCK // 2, 2 * target, 2 * target - BLOCK + 1)
    unshuffle = (wanted == source).astype(jnp.bfloat16)
    row_value = (here * band + lax.broadcasted_iota(jnp.int32, (band, 1), 0)).astype(jnp.float32)
    vertical = row_value - (height - 1) / 2.0
    vertical_square = vertical * vertical
    distance = 2.0 * width

    def xt_copy(part):
        spot = pl.ds(part * (columns // 2), columns // 2)
        return pltpu.make_async_remote_copy(
            xt.at[:, spot, pl.ds(0, rows2)],
            xt.at[:, spot, pl.ds(rows2, rows2)],
            xt_send.at[part],
            xt_recv.at[part],
            device_id=partner,
            device_id_type=MESH,
        )

    for part in range(slices):
        x_copy(part).wait()
        for block in range(part * columns // BLOCK, (part + 1) * columns // BLOCK):
            first = block * BLOCK
            column = lax.broadcasted_iota(jnp.int32, (1, BLOCK), 1).astype(jnp.float32) + (
                first - (width - 1) / 2.0
            )
            cosine = distance / jnp.sqrt(distance * distance + column * column + vertical_square)
            picked = []
            for p in range(2):
                weighted = (x_buf[p, :, first : first + BLOCK] * cosine).astype(jnp.bfloat16)
                picked.append(jnp.dot(chosen[p], weighted, preferred_element_type=jnp.float32))
            picked = jnp.concatenate(picked, axis=0).astype(jnp.bfloat16)
            turned = lax.dot_general(
                unshuffle, picked, (((1,), (1,)), ((), ())), preferred_element_type=jnp.float32
            ).astype(jnp.bfloat16)
            at = block * (BLOCK // 2)
            xt[0, at : at + BLOCK // 2, 0:rows2] = turned[: BLOCK // 2]
            xt[1, at : at + BLOCK // 2, 0:rows2] = turned[BLOCK // 2 :]
        xt_copy(part).start()

    small[0].wait_recv()
    last_input = pltpu.make_async_copy(off_recv, off_other, in_sems.at[4])
    last_input.start()
    inputs[0].wait()
    for part in range(slices):
        xt_copy(part).wait_recv()

    low = lax.broadcasted_iota(jnp.int32, (BLOCK, rows2), 1) < zdev
    te[half : half + 8, :] = jnp.zeros((8, 2 * rows2), jnp.float32)
    blocks = half // BLOCK
    for block in reversed(range(blocks)):
        start = (blocks - 1 - block) * BLOCK
        at = block * BLOCK
        for side, out in ((0, te), (1, to)):
            total = jnp.dot(
                ramp_buf[side, :, start : start + half],
                xt[1 - side],
                preferred_element_type=jnp.float32,
            )
            total = total + 0.25 * xt[side, at : at + BLOCK, :].astype(jnp.float32)
            out[at : at + BLOCK, :] = total.astype(jnp.bfloat16).astype(jnp.float32)
        for side in range(2):
            lanes = slice(side * rows2, (side + 1) * rows2)
            even = te[at : at + BLOCK, lanes]
            odd = to[at : at + BLOCK, lanes]
            later = te[at + 1 : at + 1 + BLOCK, lanes]
            turned_odd = pltpu.roll(odd, zdev, 1)
            evens = pl.ds(at, BLOCK)
            odds = pl.ds(half + at, BLOCK)
            tables[2 * side, evens, :] = jnp.where(low, even, turned_odd)
            tables[2 * side + 1, evens, :] = jnp.where(low, pltpu.roll(even, zdev, 1), odd)
            tables[2 * side, odds, :] = jnp.where(low, odd, pltpu.roll(later, zdev, 1))
            tables[2 * side + 1, odds, :] = jnp.where(low, turned_odd, later)

    for copy in inputs[2:] + [own_offsets, last_input]:
        copy.wait()
    for copy in small[1:]:
        copy.wait_recv()

    def gather(pair, first):
        base = (2 * pair + parity) * npq + first

        def rows(group, carry):
            at = pl.multiple_of(group * GROUP, GROUP)
            for r in range(GROUP):
                for q in range(4):
                    offsets = off_own if q < 2 else off_other
                    index = offsets[(q % 2) * pixels + base + at + r]
                    rows_buf[q, pl.ds(at + r, 1), :] = tables[q, pl.ds(index, 1), :]
            return carry

        lax.fori_loop(0, PIX // GROUP, rows, 0)
        total = None
        spot = pl.ds(pl.multiple_of(base, PIX), PIX)
        for q in range(4):
            turned = rows_buf[q].T
            fractions = (frac_own if q < 2 else frac_other)[pl.ds(q % 2, 1), spot]
            weight = (dist_own if q < 2 else dist_other)[pl.ds(q % 2, 1), spot]
            near = weight * (1.0 - fractions)
            far = weight * fractions
            term = near * turned[:zdev] + far * turned[zdev:]
            total = term if total is None else total + term
        return total

    def part_copy(step, piece):
        return pltpu.make_async_remote_copy(
            stage.at[step - 1, piece],
            arrived.at[step - 1, piece],
            part_send.at[step - 1, piece],
            part_recv.at[step - 1, piece],
            device_id={"angle": 2 * pair_peer(step) + parity},
            device_id_type=MESH,
        )

    def z_copy(step, piece):
        return pltpu.make_async_remote_copy(
            zstage.at[piece, band_peer(step)],
            out_ref.at[here, :, pl.ds(pl.multiple_of(piece * chunk, chunk), chunk)],
            z_send.at[step - 1, piece],
            z_recv.at[step - 1, piece],
            device_id={"rows": band_peer(step)},
            device_id_type=MESH,
        )

    def others(piece):
        for step in range(1, pairs):
            for part in range(chunk // PIX):
                at = part * PIX
                stage[step - 1, piece, :, at : at + PIX] = gather(
                    pair_peer(step), piece * chunk + at
                )
            part_copy(step, piece).start()

    def own(piece):
        for part in range(chunk // PIX):
            at = part * PIX
            mine[:, at : at + PIX] = gather(my_pair, piece * chunk + at)
        total = mine[...]
        for step in range(1, pairs):
            part_copy(step, piece).wait_recv()
            total = total + arrived[step - 1, piece]
        for b in range(bands):
            zstage[piece, b] = total[b * capacity : (b + 1) * capacity]
        for step in range(1, bands):
            z_copy(step, piece).start()
        spot = pl.ds(pl.multiple_of(piece * chunk, chunk), chunk)
        out_ref[here, :, spot] = zstage[piece, here]

    lead = min(LEAD, chunks)

    def first_pieces(piece, carry):
        others(piece)
        return carry

    def both(piece, carry):
        others(piece + lead)
        own(piece)
        return carry

    def last_pieces(piece, carry):
        own(piece)
        return carry

    lax.fori_loop(0, lead, first_pieces, 0)
    lax.fori_loop(0, chunks - lead, both, 0)
    lax.fori_loop(chunks - lead, chunks, last_pieces, 0)

    for copy in small:
        copy.wait_send()
    for part in range(slices):
        xt_copy(part).wait_send()

    def drain(piece, carry):
        for step in range(1, pairs):
            part_copy(step, piece).wait_send()
        for step in range(1, bands):
            z_copy(step, piece).wait()
        return carry

    lax.fori_loop(0, chunks, drain, 0)


def local(projections, rowmap, offsets, fractions, distance_weight):
    bands = lax.axis_size("rows")
    angles = lax.axis_size("angle")
    _, band, width = projections.shape
    planes = rowmap.shape[1]
    zdev = planes // bands
    capacity = zdev // bands
    pixels = offsets.shape[1]
    npq = pixels // angles
    pairs = angles // 2
    chunk = min(256, npq)
    chunks = npq // chunk
    half = width // 2
    ramp = jnp.asarray(odd_lag_tables(width))

    dims = (angles, bands, band, width, zdev, npq, chunk)
    vmem = pl.BlockSpec(memory_space=pltpu.VMEM)
    hbm = pl.BlockSpec(memory_space=pl.ANY)
    rows2 = 2 * zdev
    peers = max(pairs - 1, 1)
    small = pltpu.VMEM((2, pixels), jnp.float32)
    flat = (2 * pixels,)
    out = pl.pallas_call(
        functools.partial(kernel, dims),
        out_shape=jax.ShapeDtypeStruct((bands, capacity, npq), jnp.float32),
        in_specs=[hbm, vmem, hbm, hbm, hbm, hbm],
        out_specs=vmem,
        scratch_shapes=[
            pltpu.VMEM((2, band, width), jnp.float32),
            pltpu.VMEM(ramp.shape, jnp.bfloat16),
            pltpu.SMEM(flat, jnp.int32),
            pltpu.SMEM(flat, jnp.int32),
            pltpu.VMEM(flat, jnp.int32),
            pltpu.VMEM(flat, jnp.int32),
            pltpu.VMEM((2, pixels), jnp.int32),
            small,
            small,
            small,
            small,
            pltpu.VMEM((2, planes, band), jnp.float32),
            pltpu.VMEM((2, zdev, band), jnp.float32),
            pltpu.VMEM((2, half, 2 * rows2), jnp.bfloat16),
            pltpu.VMEM((half + 8, 2 * rows2), jnp.float32),
            pltpu.VMEM((half, 2 * rows2), jnp.float32),
            pltpu.VMEM((4, width, rows2), jnp.float32),
            pltpu.VMEM((4, PIX, rows2), jnp.float32),
            pltpu.VMEM((zdev, chunk), jnp.float32),
            pltpu.VMEM((peers, chunks, zdev, chunk), jnp.float32),
            pltpu.VMEM((peers, chunks, zdev, chunk), jnp.float32),
            pltpu.VMEM((chunks, bands, capacity, chunk), jnp.float32),
            pltpu.SemaphoreType.DMA((4,)),
            pltpu.SemaphoreType.DMA((6,)),
            pltpu.SemaphoreType.DMA((2, 3)),
            pltpu.SemaphoreType.DMA((4,)),
            pltpu.SemaphoreType.DMA((4,)),
            pltpu.SemaphoreType.DMA((peers, chunks)),
            pltpu.SemaphoreType.DMA((peers, chunks)),
            pltpu.SemaphoreType.DMA((max(bands - 1, 1), chunks)),
            pltpu.SemaphoreType.DMA((max(bands - 1, 1), chunks)),
        ],
        compiler_params=pltpu.CompilerParams(
            collective_id=0, has_side_effects=True, vmem_limit_bytes=56 * 1024 * 1024
        ),
    )(projections, rowmap, offsets, fractions, distance_weight, ramp)
    return out.reshape(zdev, npq)


def solution(mesh):
    in_specs = (
        P(("groups", "angle"), "rows", None),
        P(("groups", "angle"), None),
        P(("groups", "angle"), None),
        P(("groups", "angle"), None),
        P(("groups", "angle"), None),
    )
    out_specs = P(("groups", "rows"), "angle")
    return jax.shard_map(local, mesh=mesh, in_specs=in_specs, out_specs=out_specs, check_vma=False)
```

```python
import functools
import math

import jax
import jax.numpy as jnp
import ml_dtypes
import numpy as np
from jax import lax
from jax.experimental import pallas as pl
from jax.experimental.pallas import tpu as pltpu
from jax.sharding import PartitionSpec as P

BLOCK = 256
PIX = 128
GROUP = 32
LEAD = 2
LEVELS = 32767.0
MESH = pl.DeviceIdType.MESH


def ramp_values(lag):
    magnitude = np.abs(lag)
    spread = np.maximum(magnitude, 1).astype(np.float32)
    odd_term = np.float32(-1.0) / (np.float32(math.pi**2) * spread * spread)
    value = np.where(magnitude % 2 == 1, odd_term, np.float32(0.0))
    return value.astype(ml_dtypes.bfloat16)


def odd_lag_tables(width):
    half = width // 2
    blocks = half // BLOCK
    row = np.arange(BLOCK)[:, None]
    column = np.arange((2 * blocks - 1) * BLOCK)[None, :] - (blocks - 1) * BLOCK
    difference = row - column
    return np.stack([ramp_values(2 * difference - 1), ramp_values(2 * difference + 1)])


def kernel(
    dims,
    x_hbm,
    rowmap_ref,
    offsets_hbm,
    fractions_hbm,
    weight_hbm,
    ramp_hbm,
    out_ref,
    x_buf,
    ramp_buf,
    off_own,
    off_other,
    off_flat,
    off_recv,
    off_raw,
    frac_own,
    frac_other,
    dist_own,
    dist_other,
    onehot,
    select,
    xt,
    te,
    to,
    tables,
    rows_buf,
    mine,
    stage,
    arrived,
    stage_scale,
    arrived_scale,
    zstage,
    zscale,
    zgot,
    zgot_scale,
    x_sems,
    in_sems,
    small_sems,
    xt_send,
    xt_recv,
    part_send,
    part_recv,
    z_send,
    z_recv,
):
    angles, bands, band, width, zdev, npq, chunk = dims
    pairs = angles // 2
    capacity = zdev // bands
    chunks = npq // chunk
    half = width // 2
    height = band * bands
    rows2 = 2 * zdev
    slices = 4
    columns = width // slices
    me = lax.axis_index("angle")
    here = lax.axis_index("rows")
    my_pair = me // 2
    parity = me - 2 * my_pair
    partner = {"angle": 2 * my_pair + 1 - parity}

    def pair_peer(step):
        return lax.rem(my_pair + step, pairs)

    def band_peer(step):
        return lax.rem(here + step, bands)

    barrier = pltpu.get_barrier_semaphore()
    pl.semaphore_signal(barrier, inc=1, device_id=partner, device_id_type=MESH)
    for step in range(1, pairs):
        pl.semaphore_signal(
            barrier,
            inc=1,
            device_id={"angle": 2 * pair_peer(step) + parity},
            device_id_type=MESH,
        )
    for step in range(1, bands):
        pl.semaphore_signal(
            barrier, inc=1, device_id={"rows": band_peer(step)}, device_id_type=MESH
        )

    def x_copy(part):
        spot = pl.ds(part * columns, columns)
        return pltpu.make_async_copy(
            x_hbm.at[:, :, spot], x_buf.at[:, :, spot], x_sems.at[part]
        )

    for part in range(slices):
        x_copy(part).start()
    inputs = [
        pltpu.make_async_copy(ramp_hbm, ramp_buf, in_sems.at[0]),
        pltpu.make_async_copy(offsets_hbm, off_raw, in_sems.at[1]),
        pltpu.make_async_copy(fractions_hbm, frac_own, in_sems.at[2]),
        pltpu.make_async_copy(weight_hbm, dist_own, in_sems.at[3]),
    ]
    for copy in inputs:
        copy.start()

    row_of = lax.broadcasted_iota(jnp.int32, (band, rowmap_ref.shape[1]), 0) + here * band
    for p in range(2):
        hit = (rowmap_ref[p : p + 1, :] == row_of).astype(jnp.float32)
        onehot[p] = hit.T
        for slab in range(bands):
            for m in range(capacity):
                spot = slab * capacity + m
                select[p, spot : spot + 1, :] = onehot[
                    p, pl.ds(slab * zdev + here * capacity + m, 1), :
                ]
    chosen = [select[p].astype(jnp.bfloat16) for p in range(2)]

    inputs[1].wait()
    pixels = off_raw.shape[1]
    for p in range(2):
        raw = off_raw[p, :]
        off_flat[pl.ds(p * pixels, pixels)] = (raw & 1) * half + (raw >> 1)
    own_offsets = pltpu.make_async_copy(off_flat, off_own, in_sems.at[5])
    own_offsets.start()

    pl.semaphore_wait(barrier, pairs + bands - 1)

    def to_partner(src, dst, at):
        return pltpu.make_async_remote_copy(
            src,
            dst,
            small_sems.at[0, at],
            small_sems.at[1, at],
            device_id=partner,
            device_id_type=MESH,
        )

    small = [
        to_partner(off_flat, off_recv, 0),
        to_partner(fractions_hbm, frac_other, 1),
        to_partner(weight_hbm, dist_other, 2),
    ]
    for copy in small:
        copy.start()

    target = lax.broadcasted_iota(jnp.int32, (BLOCK, BLOCK), 0)
    source = lax.broadcasted_iota(jnp.int32, (BLOCK, BLOCK), 1)
    wanted = jnp.where(target < BLOCK // 2, 2 * target, 2 * target - BLOCK + 1)
    unshuffle = (wanted == source).astype(jnp.bfloat16)
    row_value = (here * band + lax.broadcasted_iota(jnp.int32, (band, 1), 0)).astype(jnp.float32)
    vertical = row_value - (height - 1) / 2.0
    vertical_square = vertical * vertical
    distance = 2.0 * width

    def xt_copy(part):
        spot = pl.ds(part * (columns // 2), columns // 2)
        return pltpu.make_async_remote_copy(
            xt.at[:, spot, pl.ds(0, rows2)],
            xt.at[:, spot, pl.ds(rows2, rows2)],
            xt_send.at[part],
            xt_recv.at[part],
            device_id=partner,
            device_id_type=MESH,
        )

    for part in range(slices):
        x_copy(part).wait()
        for block in range(part * columns // BLOCK, (part + 1) * columns // BLOCK):
            first = block * BLOCK
            column = lax.broadcasted_iota(jnp.int32, (1, BLOCK), 1).astype(jnp.float32) + (
                first - (width - 1) / 2.0
            )
            cosine = distance / jnp.sqrt(distance * distance + column * column + vertical_square)
            picked = []
            for p in range(2):
                weighted = (x_buf[p, :, first : first + BLOCK] * cosine).astype(jnp.bfloat16)
                picked.append(jnp.dot(chosen[p], weighted, preferred_element_type=jnp.float32))
            picked = jnp.concatenate(picked, axis=0).astype(jnp.bfloat16)
            turned = lax.dot_general(
                unshuffle, picked, (((1,), (1,)), ((), ())), preferred_element_type=jnp.float32
            ).astype(jnp.bfloat16)
            at = block * (BLOCK // 2)
            xt[0, at : at + BLOCK // 2, 0:rows2] = turned[: BLOCK // 2]
            xt[1, at : at + BLOCK // 2, 0:rows2] = turned[BLOCK // 2 :]
        xt_copy(part).start()

    small[0].wait_recv()
    last_input = pltpu.make_async_copy(off_recv, off_other, in_sems.at[4])
    last_input.start()
    inputs[0].wait()
    for part in range(slices):
        xt_copy(part).wait_recv()

    low = lax.broadcasted_iota(jnp.int32, (BLOCK, rows2), 1) < zdev
    te[half : half + 8, :] = jnp.zeros((8, 2 * rows2), jnp.float32)
    blocks = half // BLOCK
    for block in reversed(range(blocks)):
        start = (blocks - 1 - block) * BLOCK
        at = block * BLOCK
        for side, out in ((0, te), (1, to)):
            total = jnp.dot(
                ramp_buf[side, :, start : start + half],
                xt[1 - side],
                preferred_element_type=jnp.float32,
            )
            total = total + 0.25 * xt[side, at : at + BLOCK, :].astype(jnp.float32)
            out[at : at + BLOCK, :] = total.astype(jnp.bfloat16).astype(jnp.float32)
        for side in range(2):
            lanes = slice(side * rows2, (side + 1) * rows2)
            even = te[at : at + BLOCK, lanes]
            odd = to[at : at + BLOCK, lanes]
            later = te[at + 1 : at + 1 + BLOCK, lanes]
            turned_odd = pltpu.roll(odd, zdev, 1)
            evens = pl.ds(at, BLOCK)
            odds = pl.ds(half + at, BLOCK)
            tables[2 * side, evens, :] = jnp.where(low, even, turned_odd)
            tables[2 * side + 1, evens, :] = jnp.where(low, pltpu.roll(even, zdev, 1), odd)
            tables[2 * side, odds, :] = jnp.where(low, odd, pltpu.roll(later, zdev, 1))
            tables[2 * side + 1, odds, :] = jnp.where(low, turned_odd, later)

    for copy in inputs[2:] + [own_offsets, last_input]:
        copy.wait()
    for copy in small[1:]:
        copy.wait_recv()

    def gather(pair, first):
        base = (2 * pair + parity) * npq + first

        def rows(group, carry):
            at = pl.multiple_of(group * GROUP, GROUP)
            for r in range(GROUP):
                for q in range(4):
                    offsets = off_own if q < 2 else off_other
                    index = offsets[(q % 2) * pixels + base + at + r]
                    rows_buf[q, pl.ds(at + r, 1), :] = tables[q, pl.ds(index, 1), :]
            return carry

        lax.fori_loop(0, PIX // GROUP, rows, 0)
        total = None
        spot = pl.ds(pl.multiple_of(base, PIX), PIX)
        for q in range(4):
            turned = rows_buf[q].T
            fractions = (frac_own if q < 2 else frac_other)[pl.ds(q % 2, 1), spot]
            weight = (dist_own if q < 2 else dist_other)[pl.ds(q % 2, 1), spot]
            near = weight * (1.0 - fractions)
            far = weight * fractions
            term = near * turned[:zdev] + far * turned[zdev:]
            total = term if total is None else total + term
        return total

    def encode(values):
        most = jnp.maximum(jnp.max(jnp.abs(values), axis=0, keepdims=True), 1e-30)
        coded = jnp.round(values * (LEVELS / most)).astype(jnp.int32).astype(jnp.int16)
        return coded, most * (1.0 / LEVELS)

    def decode(coded, scale):
        return coded.astype(jnp.int32).astype(jnp.float32) * scale

    def part_copy(step, piece, which):
        src, dst = ((stage, arrived), (stage_scale, arrived_scale))[which]
        return pltpu.make_async_remote_copy(
            src.at[step - 1, piece],
            dst.at[step - 1, piece],
            part_send.at[which, step - 1, piece],
            part_recv.at[which, step - 1, piece],
            device_id={"angle": 2 * pair_peer(step) + parity},
            device_id_type=MESH,
        )

    def z_copy(step, piece, which):
        if which == 0:
            src, dst = zstage.at[piece, band_peer(step)], zgot.at[step - 1, piece]
        else:
            src, dst = zscale.at[piece], zgot_scale.at[step - 1, piece]
        return pltpu.make_async_remote_copy(
            src,
            dst,
            z_send.at[which, step - 1, piece],
            z_recv.at[which, step - 1, piece],
            device_id={"rows": band_peer(step)},
            device_id_type=MESH,
        )

    def others(piece):
        for step in range(1, pairs):
            for part in range(chunk // PIX):
                at = part * PIX
                coded, scale = encode(gather(pair_peer(step), piece * chunk + at))
                stage[step - 1, piece, :, at : at + PIX] = coded
                stage_scale[step - 1, piece, :, at : at + PIX] = scale
            for which in range(2):
                part_copy(step, piece, which).start()

    def own(piece):
        for part in range(chunk // PIX):
            at = part * PIX
            mine[:, at : at + PIX] = gather(my_pair, piece * chunk + at)
        total = mine[...]
        for step in range(1, pairs):
            for which in range(2):
                part_copy(step, piece, which).wait_recv()
            total = total + decode(arrived[step - 1, piece], arrived_scale[step - 1, piece])
        mine[...] = total
        coded, scale = encode(total)
        for b in range(bands):
            zstage[piece, b, 0:capacity] = coded[b * capacity : (b + 1) * capacity]
        zscale[piece] = scale
        for step in range(1, bands):
            for which in range(2):
                z_copy(step, piece, which).start()
        spot = pl.ds(pl.multiple_of(piece * chunk, chunk), chunk)
        at = here * capacity
        if capacity % 8 == 0:
            out_ref[here, :, spot] = mine[pl.ds(pl.multiple_of(at, 8), capacity), :]
        else:
            for m in range(capacity):
                out_ref[here, m : m + 1, spot] = mine[pl.ds(at + m, 1), :]

    lead = min(LEAD, chunks)

    def first_pieces(piece, carry):
        others(piece)
        return carry

    def both(piece, carry):
        others(piece + lead)
        own(piece)
        return carry

    def last_pieces(piece, carry):
        own(piece)
        return carry

    lax.fori_loop(0, lead, first_pieces, 0)
    lax.fori_loop(0, chunks - lead, both, 0)
    lax.fori_loop(chunks - lead, chunks, last_pieces, 0)

    for copy in small:
        copy.wait_send()
    for part in range(slices):
        xt_copy(part).wait_send()

    def drain(piece, carry):
        for which in range(2):
            for step in range(1, pairs):
                part_copy(step, piece, which).wait_send()
            for step in range(1, bands):
                z_copy(step, piece, which).wait()
        spot = pl.ds(pl.multiple_of(piece * chunk, chunk), chunk)
        for step in range(1, bands):
            source_band = lax.rem(here + bands - step, bands)
            out_ref[source_band, :, spot] = decode(
                zgot[step - 1, piece, 0:capacity], zgot_scale[step - 1, piece]
            )
        return carry

    lax.fori_loop(0, chunks, drain, 0)


def local(projections, rowmap, offsets, fractions, distance_weight):
    bands = lax.axis_size("rows")
    angles = lax.axis_size("angle")
    _, band, width = projections.shape
    planes = rowmap.shape[1]
    zdev = planes // bands
    capacity = zdev // bands
    pixels = offsets.shape[1]
    npq = pixels // angles
    pairs = angles // 2
    chunk = min(256, npq)
    chunks = npq // chunk
    half = width // 2
    ramp = jnp.asarray(odd_lag_tables(width))

    dims = (angles, bands, band, width, zdev, npq, chunk)
    vmem = pl.BlockSpec(memory_space=pltpu.VMEM)
    hbm = pl.BlockSpec(memory_space=pl.ANY)
    rows2 = 2 * zdev
    peers = max(pairs - 1, 1)
    others = max(bands - 1, 1)
    padded = -(-capacity // 16) * 16
    small = pltpu.VMEM((2, pixels), jnp.float32)
    flat = (2 * pixels,)
    out = pl.pallas_call(
        functools.partial(kernel, dims),
        out_shape=jax.ShapeDtypeStruct((bands, capacity, npq), jnp.float32),
        in_specs=[hbm, vmem, hbm, hbm, hbm, hbm],
        out_specs=vmem,
        scratch_shapes=[
            pltpu.VMEM((2, band, width), jnp.float32),
            pltpu.VMEM(ramp.shape, jnp.bfloat16),
            pltpu.SMEM(flat, jnp.int32),
            pltpu.SMEM(flat, jnp.int32),
            pltpu.VMEM(flat, jnp.int32),
            pltpu.VMEM(flat, jnp.int32),
            pltpu.VMEM((2, pixels), jnp.int32),
            small,
            small,
            small,
            small,
            pltpu.VMEM((2, planes, band), jnp.float32),
            pltpu.VMEM((2, zdev, band), jnp.float32),
            pltpu.VMEM((2, half, 2 * rows2), jnp.bfloat16),
            pltpu.VMEM((half + 8, 2 * rows2), jnp.float32),
            pltpu.VMEM((half, 2 * rows2), jnp.float32),
            pltpu.VMEM((4, width, rows2), jnp.float32),
            pltpu.VMEM((4, PIX, rows2), jnp.float32),
            pltpu.VMEM((zdev, chunk), jnp.float32),
            pltpu.VMEM((peers, chunks, zdev, chunk), jnp.int16),
            pltpu.VMEM((peers, chunks, zdev, chunk), jnp.int16),
            pltpu.VMEM((peers, chunks, 1, chunk), jnp.float32),
            pltpu.VMEM((peers, chunks, 1, chunk), jnp.float32),
            pltpu.VMEM((chunks, bands, padded, chunk), jnp.int16),
            pltpu.VMEM((chunks, 1, chunk), jnp.float32),
            pltpu.VMEM((others, chunks, padded, chunk), jnp.int16),
            pltpu.VMEM((others, chunks, 1, chunk), jnp.float32),
            pltpu.SemaphoreType.DMA((4,)),
            pltpu.SemaphoreType.DMA((6,)),
            pltpu.SemaphoreType.DMA((2, 3)),
            pltpu.SemaphoreType.DMA((4,)),
            pltpu.SemaphoreType.DMA((4,)),
            pltpu.SemaphoreType.DMA((2, peers, chunks)),
            pltpu.SemaphoreType.DMA((2, peers, chunks)),
            pltpu.SemaphoreType.DMA((2, others, chunks)),
            pltpu.SemaphoreType.DMA((2, others, chunks)),
        ],
        compiler_params=pltpu.CompilerParams(
            collective_id=0, has_side_effects=True, vmem_limit_bytes=56 * 1024 * 1024
        ),
    )(projections, rowmap, offsets, fractions, distance_weight, ramp)
    return out.reshape(zdev, npq)


def solution(mesh):
    in_specs = (
        P(("groups", "angle"), "rows", None),
        P(("groups", "angle"), None),
        P(("groups", "angle"), None),
        P(("groups", "angle"), None),
        P(("groups", "angle"), None),
    )
    out_specs = P(("groups", "rows"), "angle")
    return jax.shard_map(local, mesh=mesh, in_specs=in_specs, out_specs=out_specs, check_vma=False)
```

```python
import functools
import math

import jax
import jax.numpy as jnp
import ml_dtypes
import numpy as np
from jax import lax
from jax.experimental import pallas as pl
from jax.experimental.pallas import tpu as pltpu
from jax.sharding import PartitionSpec as P

BLOCK = 256
PIX = 128
GROUP = 32
LEAD = 1
LEVELS = 32767.0
MESH = pl.DeviceIdType.MESH


def ramp_values(lag):
    magnitude = np.abs(lag)
    spread = np.maximum(magnitude, 1).astype(np.float32)
    odd_term = np.float32(-1.0) / (np.float32(math.pi**2) * spread * spread)
    value = np.where(magnitude % 2 == 1, odd_term, np.float32(0.0))
    return value.astype(ml_dtypes.bfloat16)


def odd_lag_tables(width):
    half = width // 2
    blocks = half // BLOCK
    row = np.arange(BLOCK)[:, None]
    column = np.arange((2 * blocks - 1) * BLOCK)[None, :] - (blocks - 1) * BLOCK
    difference = row - column
    return np.stack([ramp_values(2 * difference - 1), ramp_values(2 * difference + 1)])


def kernel(
    dims,
    x_hbm,
    rowmap_ref,
    offsets_hbm,
    fractions_hbm,
    weight_hbm,
    ramp_hbm,
    out_ref,
    x_buf,
    ramp_buf,
    off_own,
    off_other,
    off_flat,
    off_recv,
    off_raw,
    frac_own,
    frac_other,
    dist_own,
    dist_other,
    onehot,
    select,
    xt,
    te,
    to,
    tables,
    rows_buf,
    mine,
    stage,
    arrived,
    stage_scale,
    arrived_scale,
    zstage,
    zscale,
    zgot,
    zgot_scale,
    x_sems,
    in_sems,
    small_sems,
    xt_send,
    xt_recv,
    part_send,
    part_recv,
    z_send,
    z_recv,
):
    angles, bands, band, width, zdev, npq, chunk = dims
    pairs = angles // 2
    capacity = zdev // bands
    chunks = npq // chunk
    half = width // 2
    height = band * bands
    rows2 = 2 * zdev
    slices = 4
    columns = width // slices
    me = lax.axis_index("angle")
    here = lax.axis_index("rows")
    my_pair = me // 2
    parity = me - 2 * my_pair
    partner = {"angle": 2 * my_pair + 1 - parity}

    def pair_peer(step):
        return lax.rem(my_pair + step, pairs)

    def band_peer(step):
        return lax.rem(here + step, bands)

    barrier = pltpu.get_barrier_semaphore()
    pl.semaphore_signal(barrier, inc=1, device_id=partner, device_id_type=MESH)
    for step in range(1, pairs):
        pl.semaphore_signal(
            barrier,
            inc=1,
            device_id={"angle": 2 * pair_peer(step) + parity},
            device_id_type=MESH,
        )
    for step in range(1, bands):
        pl.semaphore_signal(
            barrier, inc=1, device_id={"rows": band_peer(step)}, device_id_type=MESH
        )

    def x_copy(part):
        spot = pl.ds(part * columns, columns)
        return pltpu.make_async_copy(
            x_hbm.at[:, :, spot], x_buf.at[:, :, spot], x_sems.at[part]
        )

    for part in range(slices):
        x_copy(part).start()
    inputs = [
        pltpu.make_async_copy(ramp_hbm, ramp_buf, in_sems.at[0]),
        pltpu.make_async_copy(offsets_hbm, off_raw, in_sems.at[1]),
        pltpu.make_async_copy(fractions_hbm, frac_own, in_sems.at[2]),
        pltpu.make_async_copy(weight_hbm, dist_own, in_sems.at[3]),
    ]
    for copy in inputs:
        copy.start()

    row_of = lax.broadcasted_iota(jnp.int32, (band, rowmap_ref.shape[1]), 0) + here * band
    for p in range(2):
        hit = (rowmap_ref[p : p + 1, :] == row_of).astype(jnp.float32)
        onehot[p] = hit.T
        for slab in range(bands):
            for m in range(capacity):
                spot = slab * capacity + m
                select[p, spot : spot + 1, :] = onehot[
                    p, pl.ds(slab * zdev + here * capacity + m, 1), :
                ]
    chosen = [select[p].astype(jnp.bfloat16) for p in range(2)]

    inputs[1].wait()
    pixels = off_raw.shape[1]
    for p in range(2):
        raw = off_raw[p, :]
        off_flat[pl.ds(p * pixels, pixels)] = (raw & 1) * half + (raw >> 1)
    own_offsets = pltpu.make_async_copy(off_flat, off_own, in_sems.at[5])
    own_offsets.start()

    pl.semaphore_wait(barrier, pairs + bands - 1)

    def to_partner(src, dst, at):
        return pltpu.make_async_remote_copy(
            src,
            dst,
            small_sems.at[0, at],
            small_sems.at[1, at],
            device_id=partner,
            device_id_type=MESH,
        )

    small = [
        to_partner(off_flat, off_recv, 0),
        to_partner(fractions_hbm, frac_other, 1),
        to_partner(weight_hbm, dist_other, 2),
    ]
    for copy in small:
        copy.start()

    target = lax.broadcasted_iota(jnp.int32, (BLOCK, BLOCK), 0)
    source = lax.broadcasted_iota(jnp.int32, (BLOCK, BLOCK), 1)
    wanted = jnp.where(target < BLOCK // 2, 2 * target, 2 * target - BLOCK + 1)
    unshuffle = (wanted == source).astype(jnp.bfloat16)
    row_value = (here * band + lax.broadcasted_iota(jnp.int32, (band, 1), 0)).astype(jnp.float32)
    vertical = row_value - (height - 1) / 2.0
    vertical_square = vertical * vertical
    distance = 2.0 * width

    def xt_copy(part):
        spot = pl.ds(part * (columns // 2), columns // 2)
        return pltpu.make_async_remote_copy(
            xt.at[:, spot, pl.ds(0, rows2)],
            xt.at[:, spot, pl.ds(rows2, rows2)],
            xt_send.at[part],
            xt_recv.at[part],
            device_id=partner,
            device_id_type=MESH,
        )

    for part in range(slices):
        x_copy(part).wait()
        for block in range(part * columns // BLOCK, (part + 1) * columns // BLOCK):
            first = block * BLOCK
            column = lax.broadcasted_iota(jnp.int32, (1, BLOCK), 1).astype(jnp.float32) + (
                first - (width - 1) / 2.0
            )
            cosine = distance / jnp.sqrt(distance * distance + column * column + vertical_square)
            picked = []
            for p in range(2):
                weighted = (x_buf[p, :, first : first + BLOCK] * cosine).astype(jnp.bfloat16)
                picked.append(jnp.dot(chosen[p], weighted, preferred_element_type=jnp.float32))
            picked = jnp.concatenate(picked, axis=0).astype(jnp.bfloat16)
            turned = lax.dot_general(
                unshuffle, picked, (((1,), (1,)), ((), ())), preferred_element_type=jnp.float32
            ).astype(jnp.bfloat16)
            at = block * (BLOCK // 2)
            xt[0, at : at + BLOCK // 2, 0:rows2] = turned[: BLOCK // 2]
            xt[1, at : at + BLOCK // 2, 0:rows2] = turned[BLOCK // 2 :]
        xt_copy(part).start()

    small[0].wait_recv()
    last_input = pltpu.make_async_copy(off_recv, off_other, in_sems.at[4])
    last_input.start()
    inputs[0].wait()
    for part in range(slices):
        xt_copy(part).wait_recv()

    low = lax.broadcasted_iota(jnp.int32, (BLOCK, rows2), 1) < zdev
    te[half : half + 8, :] = jnp.zeros((8, 2 * rows2), jnp.float32)
    blocks = half // BLOCK
    for block in reversed(range(blocks)):
        start = (blocks - 1 - block) * BLOCK
        at = block * BLOCK
        for side, out in ((0, te), (1, to)):
            total = jnp.dot(
                ramp_buf[side, :, start : start + half],
                xt[1 - side],
                preferred_element_type=jnp.float32,
            )
            total = total + 0.25 * xt[side, at : at + BLOCK, :].astype(jnp.float32)
            out[at : at + BLOCK, :] = total.astype(jnp.bfloat16).astype(jnp.float32)
        for side in range(2):
            lanes = slice(side * rows2, (side + 1) * rows2)
            even = te[at : at + BLOCK, lanes]
            odd = to[at : at + BLOCK, lanes]
            later = te[at + 1 : at + 1 + BLOCK, lanes]
            turned_odd = pltpu.roll(odd, zdev, 1)
            evens = pl.ds(at, BLOCK)
            odds = pl.ds(half + at, BLOCK)
            tables[2 * side, evens, :] = jnp.where(low, even, turned_odd)
            tables[2 * side + 1, evens, :] = jnp.where(low, pltpu.roll(even, zdev, 1), odd)
            tables[2 * side, odds, :] = jnp.where(low, odd, pltpu.roll(later, zdev, 1))
            tables[2 * side + 1, odds, :] = jnp.where(low, turned_odd, later)

    for copy in inputs[2:] + [own_offsets, last_input]:
        copy.wait()
    for copy in small[1:]:
        copy.wait_recv()

    def gather(pair, first):
        base = (2 * pair + parity) * npq + first

        def rows(group, carry):
            at = pl.multiple_of(group * GROUP, GROUP)
            for r in range(GROUP):
                for q in range(4):
                    offsets = off_own if q < 2 else off_other
                    index = offsets[(q % 2) * pixels + base + at + r]
                    rows_buf[q, pl.ds(at + r, 1), :] = tables[q, pl.ds(index, 1), :]
            return carry

        lax.fori_loop(0, PIX // GROUP, rows, 0)
        total = None
        spot = pl.ds(pl.multiple_of(base, PIX), PIX)
        for q in range(4):
            turned = rows_buf[q].T
            fractions = (frac_own if q < 2 else frac_other)[pl.ds(q % 2, 1), spot]
            weight = (dist_own if q < 2 else dist_other)[pl.ds(q % 2, 1), spot]
            near = weight * (1.0 - fractions)
            far = weight * fractions
            term = near * turned[:zdev] + far * turned[zdev:]
            total = term if total is None else total + term
        return total

    def encode(values):
        most = jnp.maximum(jnp.max(jnp.abs(values), axis=0, keepdims=True), 1e-30)
        coded = jnp.round(values * (LEVELS / most)).astype(jnp.int32).astype(jnp.int16)
        return coded, most * (1.0 / LEVELS)

    def decode(coded, scale):
        return coded.astype(jnp.int32).astype(jnp.float32) * scale

    def part_copy(step, piece, which):
        src, dst = ((stage, arrived), (stage_scale, arrived_scale))[which]
        return pltpu.make_async_remote_copy(
            src.at[step - 1, piece],
            dst.at[step - 1, piece],
            part_send.at[which, step - 1, piece],
            part_recv.at[which, step - 1, piece],
            device_id={"angle": 2 * pair_peer(step) + parity},
            device_id_type=MESH,
        )

    def z_copy(step, piece, which):
        if which == 0:
            src, dst = zstage.at[piece, band_peer(step)], zgot.at[step - 1, piece]
        else:
            src, dst = zscale.at[piece], zgot_scale.at[step - 1, piece]
        return pltpu.make_async_remote_copy(
            src,
            dst,
            z_send.at[which, step - 1, piece],
            z_recv.at[which, step - 1, piece],
            device_id={"rows": band_peer(step)},
            device_id_type=MESH,
        )

    def others(piece):
        for step in range(1, pairs):
            for part in range(chunk // PIX):
                at = part * PIX
                coded, scale = encode(gather(pair_peer(step), piece * chunk + at))
                stage[step - 1, piece, :, at : at + PIX] = coded
                stage_scale[step - 1, piece, :, at : at + PIX] = scale
            for which in range(2):
                part_copy(step, piece, which).start()

    def own(piece):
        for part in range(chunk // PIX):
            at = part * PIX
            mine[:, at : at + PIX] = gather(my_pair, piece * chunk + at)
        total = mine[...]
        for step in range(1, pairs):
            for which in range(2):
                part_copy(step, piece, which).wait_recv()
            total = total + decode(arrived[step - 1, piece], arrived_scale[step - 1, piece])
        mine[...] = total
        coded, scale = encode(total)
        for b in range(bands):
            zstage[piece, b, 0:capacity] = coded[b * capacity : (b + 1) * capacity]
        zscale[piece] = scale
        for step in range(1, bands):
            for which in range(2):
                z_copy(step, piece, which).start()
        spot = pl.ds(pl.multiple_of(piece * chunk, chunk), chunk)
        at = here * capacity
        if capacity % 8 == 0:
            out_ref[here, :, spot] = mine[pl.ds(pl.multiple_of(at, 8), capacity), :]
        else:
            for m in range(capacity):
                out_ref[here, m : m + 1, spot] = mine[pl.ds(at + m, 1), :]

    lead = min(LEAD, chunks)

    def first_pieces(piece, carry):
        others(piece)
        return carry

    def both(piece, carry):
        others(piece + lead)
        own(piece)
        return carry

    def last_pieces(piece, carry):
        own(piece)
        return carry

    lax.fori_loop(0, lead, first_pieces, 0)
    lax.fori_loop(0, chunks - lead, both, 0)
    lax.fori_loop(chunks - lead, chunks, last_pieces, 0)

    for copy in small:
        copy.wait_send()
    for part in range(slices):
        xt_copy(part).wait_send()

    def drain(piece, carry):
        for which in range(2):
            for step in range(1, pairs):
                part_copy(step, piece, which).wait_send()
            for step in range(1, bands):
                z_copy(step, piece, which).wait()
        spot = pl.ds(pl.multiple_of(piece * chunk, chunk), chunk)
        for step in range(1, bands):
            source_band = lax.rem(here + bands - step, bands)
            out_ref[source_band, :, spot] = decode(
                zgot[step - 1, piece, 0:capacity], zgot_scale[step - 1, piece]
            )
        return carry

    lax.fori_loop(0, chunks, drain, 0)


def local(projections, rowmap, offsets, fractions, distance_weight):
    bands = lax.axis_size("rows")
    angles = lax.axis_size("angle")
    _, band, width = projections.shape
    planes = rowmap.shape[1]
    zdev = planes // bands
    capacity = zdev // bands
    pixels = offsets.shape[1]
    npq = pixels // angles
    pairs = angles // 2
    chunk = min(512, npq)
    chunks = npq // chunk
    half = width // 2
    ramp = jnp.asarray(odd_lag_tables(width))

    dims = (angles, bands, band, width, zdev, npq, chunk)
    vmem = pl.BlockSpec(memory_space=pltpu.VMEM)
    hbm = pl.BlockSpec(memory_space=pl.ANY)
    rows2 = 2 * zdev
    peers = max(pairs - 1, 1)
    others = max(bands - 1, 1)
    padded = -(-capacity // 16) * 16
    small = pltpu.VMEM((2, pixels), jnp.float32)
    flat = (2 * pixels,)
    out = pl.pallas_call(
        functools.partial(kernel, dims),
        out_shape=jax.ShapeDtypeStruct((bands, capacity, npq), jnp.float32),
        in_specs=[hbm, vmem, hbm, hbm, hbm, hbm],
        out_specs=vmem,
        scratch_shapes=[
            pltpu.VMEM((2, band, width), jnp.float32),
            pltpu.VMEM(ramp.shape, jnp.bfloat16),
            pltpu.SMEM(flat, jnp.int32),
            pltpu.SMEM(flat, jnp.int32),
            pltpu.VMEM(flat, jnp.int32),
            pltpu.VMEM(flat, jnp.int32),
            pltpu.VMEM((2, pixels), jnp.int32),
            small,
            small,
            small,
            small,
            pltpu.VMEM((2, planes, band), jnp.float32),
            pltpu.VMEM((2, zdev, band), jnp.float32),
            pltpu.VMEM((2, half, 2 * rows2), jnp.bfloat16),
            pltpu.VMEM((half + 8, 2 * rows2), jnp.float32),
            pltpu.VMEM((half, 2 * rows2), jnp.float32),
            pltpu.VMEM((4, width, rows2), jnp.float32),
            pltpu.VMEM((4, PIX, rows2), jnp.float32),
            pltpu.VMEM((zdev, chunk), jnp.float32),
            pltpu.VMEM((peers, chunks, zdev, chunk), jnp.int16),
            pltpu.VMEM((peers, chunks, zdev, chunk), jnp.int16),
            pltpu.VMEM((peers, chunks, 1, chunk), jnp.float32),
            pltpu.VMEM((peers, chunks, 1, chunk), jnp.float32),
            pltpu.VMEM((chunks, bands, padded, chunk), jnp.int16),
            pltpu.VMEM((chunks, 1, chunk), jnp.float32),
            pltpu.VMEM((others, chunks, padded, chunk), jnp.int16),
            pltpu.VMEM((others, chunks, 1, chunk), jnp.float32),
            pltpu.SemaphoreType.DMA((4,)),
            pltpu.SemaphoreType.DMA((6,)),
            pltpu.SemaphoreType.DMA((2, 3)),
            pltpu.SemaphoreType.DMA((4,)),
            pltpu.SemaphoreType.DMA((4,)),
            pltpu.SemaphoreType.DMA((2, peers, chunks)),
            pltpu.SemaphoreType.DMA((2, peers, chunks)),
            pltpu.SemaphoreType.DMA((2, others, chunks)),
            pltpu.SemaphoreType.DMA((2, others, chunks)),
        ],
        compiler_params=pltpu.CompilerParams(
            collective_id=0, has_side_effects=True, vmem_limit_bytes=56 * 1024 * 1024
        ),
    )(projections, rowmap, offsets, fractions, distance_weight, ramp)
    return out.reshape(zdev, npq)


def solution(mesh):
    in_specs = (
        P(("groups", "angle"), "rows", None),
        P(("groups", "angle"), None),
        P(("groups", "angle"), None),
        P(("groups", "angle"), None),
        P(("groups", "angle"), None),
    )
    out_specs = P(("groups", "rows"), "angle")
    return jax.shard_map(local, mesh=mesh, in_specs=in_specs, out_specs=out_specs, check_vma=False)
```
